32 devices in a mesh: replica: 2 (over x), tensor: 16 (over z, y, core).
Axes of the slice: x: 2, y: 2, z: 4, core: 2. Of those that a mesh axis runs over, the one named last changes fastest.
Arguments:
- tokens: bfloat16 [512, 8192], P('replica', 'tensor'), parts along dimension 0, may hold values from -6 to 6
- gate_matrix: bfloat16 [8192, 28672], P(None, 'tensor'), may hold values from -0.0625 to 0.0625
- up_matrix: bfloat16 [8192, 28672], P(None, 'tensor'), may hold values from -0.0625 to 0.0625
- down_matrix: bfloat16 [28672, 8192], P('tensor'), may hold values from -0.046875 to 0.046875
- adapter_shrink_factors: bfloat16 [16, 16, 28672], P('tensor'), may hold values from -0.03125 to 0.03125
- adapter_expand_factors: bfloat16 [16, 16, 8192], P('tensor'), may hold values from -1.5 to 1.5
- request_adapter_ids: int32 [512, 1], P('replica'), parts along dimension 0, may hold values from 0 to 15
- adapter_store_row: int32 [16], replicated, may hold values from 0 to 15, each once
Outputs:
- mixed: bfloat16 [512, 8192], P('replica', 'tensor'), parts along dimension 0
The draws below stay inside these ranges and needn't reach their ends.
There are 2 independent parts, one for each index of `replica`. The reference program is written for one: setup_inputs(seed, part) draws one part's arguments, and reference() takes and returns one part's arrays. A program takes and returns all parts, laid end to end along the dimension named above; an argument that names none is the same for every part. Nothing has to cross between parts.
Inputs may be any that keep to these rules, and one draw needn't show every extreme that they name: `request_adapter_ids`: every one of the 16 adapter ids is named by at least one row. `adapter_store_row`: A permutation: each store row holds exactly one adapter.
All inputs are finite; a program needn't handle non-finite values.
Results may differ from the reference program's by a relative error of at most 0.0051.
Values may be sent and summed in bfloat16 or wider, within the bound.
A program may use at most 256 MiB of HBM per device.

```python
import jax
import jax.numpy as jnp
from jax import lax

MODEL_WIDTH = 8192
HIDDEN_UNITS = 28672
ADAPTER_RANK = 16
ROWS = 256
ADAPTER_COUNT = 16


def strengthened(drawn, key, source, target, blocks, factor):
    owner, partner = [(jnp.arange(drawn.shape[axis_at]) // (drawn.shape[axis_at] // blocks)).reshape([-1 if axis == axis_at else 1 for axis in range(drawn.ndim)]) for axis_at in (source, target)]
    chosen = jax.random.permutation(key, blocks)[partner]
    strong = (owner == chosen) | (owner == (partner + blocks // 2) % blocks)
    return jnp.where(strong, factor * drawn, drawn)


def block_scale(rng, dims, pieces, low, largest):
    def one(dim, blocks):
        heights = jax.random.uniform(jax.random.fold_in(jax.random.fold_in(rng, 6), dim), (blocks,), jnp.float32, low / len(pieces), largest / len(pieces))
        return jnp.repeat(jnp.exp(heights), dims[dim] // blocks).reshape((-1,) + (1,) * (len(dims) - dim - 1))

    level = one(*pieces[0])
    for cut in pieces[1:]:
        level = level * one(*cut)
    return level


def different_ones(rng, rows, count, top, lift):
    sequence = jax.random.permutation(jax.random.fold_in(rng, 1), count)
    pull = sequence
    for power in range(3):
        pull = pull * pull // count
    pull = pull * lift // count
    chance = jax.random.randint(jax.random.fold_in(rng, 2), (rows, count), 0, 4096) + pull
    sure = jax.random.permutation(jax.random.fold_in(rng, 3), rows)[jnp.arange(count) % rows]
    chance = jnp.where(jnp.arange(rows)[:, None] == sure[None, :], 1 << 14, chance)
    priority = chance * count + jnp.arange(count)
    return lax.top_k(priority.astype(jnp.int32), top)[1].astype(jnp.int32)


def centred(rng, dims, spread, reach, cuts=(), held_as=jnp.bfloat16):
    gain = block_scale(rng, dims, cuts, -0.22, 0.18) if cuts else 1.0
    array = jax.random.normal(rng, dims, jnp.float32) * spread * gain
    return jnp.minimum(jnp.maximum(array, -reach), reach).astype(held_as)


def bell_draw_with(own_key, shape, deviation, limit, pieces, heavy, kind=jnp.bfloat16):
    result = deviation * jax.random.normal(own_key, shape, jnp.float32)
    if pieces:
        result = result * block_scale(own_key, shape, pieces, -0.22, 0.18)
    return jnp.clip(strengthened(result, jax.random.fold_in(own_key, 3), *heavy), -limit, limit).astype(kind)


def setup_inputs(seed: int = 0, part: int = 0) -> dict:
    keys = jax.random.split(jax.random.key(seed), 9)
    own_keys = jax.random.split(jax.random.fold_in(keys[8], part), 9)
    return {
        "tokens": centred(own_keys[0], (ROWS, MODEL_WIDTH), 1.0, 6.0, ((1, 16),)),
        "gate_matrix": centred(keys[1], (MODEL_WIDTH, HIDDEN_UNITS), MODEL_WIDTH ** -0.5, 0.0625, ((1, 16),)),
        "up_matrix": centred(keys[2], (MODEL_WIDTH, HIDDEN_UNITS), MODEL_WIDTH ** -0.5, 0.0625, ((1, 16),)),
        "down_matrix": bell_draw_with(keys[3], (HIDDEN_UNITS, MODEL_WIDTH), HIDDEN_UNITS ** -0.5, 0.046875, ((0, 16),), (0, 1, 16, 2.0)),
        "adapter_shrink_factors": centred(keys[4], (ADAPTER_COUNT, ADAPTER_RANK, HIDDEN_UNITS), HIDDEN_UNITS ** -0.5, 0.03125, ((0, 16),)),
        "adapter_expand_factors": centred(keys[5], (ADAPTER_COUNT, ADAPTER_RANK, MODEL_WIDTH), ADAPTER_RANK ** -0.5, 1.5, ((0, 16),)),
        "request_adapter_ids": different_ones(own_keys[6], ROWS, ADAPTER_COUNT, 1, 1024),
        "adapter_store_row": jax.random.permutation(keys[7], ADAPTER_COUNT).astype(jnp.int32),
    }


adapter_scale = 2.0


def reference(tokens, gate_matrix, up_matrix, down_matrix, adapter_shrink_factors, adapter_expand_factors, request_adapter_ids, adapter_store_row):
    gate_proj = jnp.dot(tokens, gate_matrix, preferred_element_type=jnp.float32)
    up_proj = jnp.dot(tokens, up_matrix, preferred_element_type=jnp.float32)
    hidden = (jax.nn.silu(gate_proj) * up_proj).astype(jnp.bfloat16)
    base_output = jnp.dot(hidden, down_matrix, preferred_element_type=jnp.float32)
    store_row_ids = adapter_store_row[request_adapter_ids[:, 0].astype(jnp.int32)].astype(jnp.int32)
    flattened_shrink = adapter_shrink_factors.reshape(ADAPTER_COUNT * ADAPTER_RANK, HIDDEN_UNITS)
    all_shrink = jnp.dot(hidden, flattened_shrink.T, preferred_element_type=jnp.float32).reshape(ROWS, ADAPTER_COUNT, ADAPTER_RANK)
    shrink_product = jnp.take_along_axis(all_shrink, store_row_ids[:, None, None], axis=1)[:, 0, :]
    expand_factor_rows = adapter_expand_factors[store_row_ids].astype(jnp.float32)
    adapter_delta = jnp.einsum("ya,yaf->yf", shrink_product.astype(jnp.float32), expand_factor_rows)
    return (base_output + adapter_scale * adapter_delta).astype(jnp.bfloat16)
```

```python
import functools

import jax
import jax.numpy as jnp
from jax import lax
from jax.experimental import pallas as pl
from jax.experimental.pallas import tpu as pltpu
from jax.sharding import PartitionSpec as P

adapter_scale = 2.0


def local(
    tokens,
    gate_matrix,
    up_matrix,
    down_matrix,
    adapter_shrink_factors,
    adapter_expand_factors,
    request_adapter_ids,
    adapter_store_row,
):
    row_count = tokens.shape[0]
    feature_piece = lax.all_gather(tokens, "tensor", axis=1, tiled=True)
    gate_proj = jnp.dot(feature_piece, gate_matrix, preferred_element_type=jnp.float32)
    up_proj = jnp.dot(feature_piece, up_matrix, preferred_element_type=jnp.float32)
    hidden = (jax.nn.silu(gate_proj) * up_proj).astype(jnp.bfloat16)
    shrink_pages, expand_pages = (
        lax.all_to_all(adapter_shrink_factors, "tensor", split_axis=2, concat_axis=0, tiled=True),
        lax.all_to_all(adapter_expand_factors, "tensor", split_axis=2, concat_axis=0, tiled=True),
    )
    store_count = shrink_pages.shape[0]
    rank_size = shrink_pages.shape[1]
    store_row_ids = adapter_store_row[request_adapter_ids[:, 0]]
    selector = (store_row_ids[:, None] == jnp.arange(store_count, dtype=jnp.int32)[None, :]).astype(
        jnp.float32
    )
    flat_shrink = shrink_pages.reshape(store_count * rank_size, shrink_pages.shape[2])
    every_shrink = jnp.dot(hidden, flat_shrink.T, preferred_element_type=jnp.float32).reshape(
        row_count, store_count, rank_size
    )
    shrink_part = jnp.sum(every_shrink * selector[:, :, None], axis=1)
    shrink_product = lax.psum(shrink_part, "tensor")
    spread_shrink = (selector[:, :, None] * shrink_product[:, None, :]).reshape(
        row_count, store_count * rank_size
    )
    flat_expand = expand_pages.reshape(store_count * rank_size, expand_pages.shape[2]).astype(
        jnp.float32
    )
    adapter_delta = jnp.dot(
        spread_shrink,
        flat_expand,
        precision=lax.Precision.HIGHEST,
        preferred_element_type=jnp.float32,
    )
    partial_out = jnp.dot(hidden, down_matrix, preferred_element_type=jnp.float32)
    base_output = lax.psum_scatter(partial_out, "tensor", scatter_dimension=1, tiled=True)
    return (base_output + adapter_scale * adapter_delta).astype(jnp.bfloat16)


layers = 4
group = 16
weight_slots = 3
down_slots = 6
f32 = jnp.float32
bf16 = jnp.bfloat16
NT = (((1,), (1,)), ((), ()))


def near_first(z, j):
    low = jnp.where(z == 0, j, jnp.where(j < 2, 1 - j, j))
    w = 3 - z
    high = jnp.where(w == 0, j, jnp.where(j < 2, 1 - j, j))
    return jnp.where(z < 2, low, 3 - high)


def fused(
    tokens, gate, up, down, shrink, expand, ids, store_row, out,
    tok, gate_w, up_w, down_w, gate_acc, up_acc, hid, pages, expand_pages,
    core_send, core_recv, keep, y_send, y_recv, z_send, up_recv, dn_recv, sh_send, sh_recv,
    tok_recv_sem, tok_core_sem, tok_y_sem, tok_up_sem, tok_dn_sem, own_sem,
    gate_sem, up_sem, down_sem,
    core_s, core_r, y_s, y_r, z_s, up_r, dn_r,
    page_s, page_r, exp_s, exp_r, sh_s, sh_r,
):
    me = lax.axis_index("tensor")
    c, y, z = me % 2, (me // 2) % 2, me // 4
    piece = tokens.shape[1]
    units = hid.shape[1]
    rows = tokens.shape[0]
    rank = shrink.shape[1]

    def dev(z_, y_, c_):
        return {"tensor": 4 * z_ + 2 * y_ + c_}

    core_dev = dev(z, y, 1 - c)
    y_dev = dev(z, 1 - y, c)
    above = dev(jnp.minimum(z + 1, 3), y, c)
    below = dev(jnp.maximum(z - 1, 0), y, c)

    def remote(src, dst, s, r, device):
        return pltpu.make_async_remote_copy(
            src_ref=src, dst_ref=dst, send_sem=s, recv_sem=r,
            device_id=device, device_id_type=pl.DeviceIdType.MESH)

    def pair_of(step):
        second = jnp.where(step == 0, 0, jnp.where(step == 7, 1, 1 - step % 2))
        at = jnp.where(step == 7, 3, jnp.where(step % 2 == 1, (step + 1) // 2, jnp.maximum(step // 2 - 1, 0)))
        y_ = jnp.where(second == 1, 1 - y, y)
        return 2 * near_first(z, at) + y_

    def weights(step):
        slot = step % weight_slots
        at = pl.ds(pl.multiple_of(pair_of(step) * 2 * piece, 2 * piece), 2 * piece)
        return (
            pltpu.make_async_copy(gate.at[at, :], gate_w.at[slot], gate_sem.at[slot]),
            pltpu.make_async_copy(up.at[at, :], up_w.at[slot], up_sem.at[slot]),
        )

    def target(q):
        g, sub = q // 2, q % 2
        z_ = near_first(z, 3 - g % 4)
        y_ = jnp.where(g < 4, 1 - y, y)
        c_ = jnp.where(sub == 0, 1 - c, c)
        return 4 * z_ + 2 * y_ + c_

    def down_copy(q):
        slot = q % down_slots
        at = pl.ds(pl.multiple_of(target(q) * piece, piece), piece)
        return pltpu.make_async_copy(down.at[:, at], down_w.at[slot], down_sem.at[slot])

    for step in range(weight_slots):
        for copy in weights(step):
            copy.start()

    barrier = pltpu.get_barrier_semaphore()

    @pl.loop(1, group)
    def _(i):
        pl.semaphore_signal(barrier, inc=1, device_id={"tensor": (me + i) % group}, device_id_type=pl.DeviceIdType.MESH)

    pl.semaphore_wait(barrier, group - 1)

    def block(z_, y_, c_):
        return tok.at[2 * z_ + y_, :, pl.ds(pl.multiple_of(c_ * piece, piece), piece)]

    def tok_copy(z_, y_, c_, sem, device, src=None):
        ref = block(z_, y_, c_)
        t = 4 * z_ + 2 * y_ + c_
        return remote(ref if src is None else src, ref, sem, tok_recv_sem.at[t], device)

    def to_core(z_, y_, src=None):
        return tok_copy(z_, y_, c, tok_core_sem.at[2 * z_ + y_], core_dev, src)

    def to_y(z_, src=None):
        return tok_copy(z_, y, c, tok_y_sem.at[z_], y_dev, src)

    def to_up(z_, src=None):
        return tok_copy(z_, y, c, tok_up_sem.at[z_], above, src)

    def to_dn(z_, src=None):
        return tok_copy(z_, y, c, tok_dn_sem.at[z_], below, src)

    def arrived(z_, y_, c_):
        tok_copy(z_, y_, c_, tok_up_sem.at[0], core_dev).wait_recv()

    @pl.when(z < 3)
    def _():
        to_up(z, tokens).start()

    @pl.when(z > 0)
    def _():
        to_dn(z, tokens).start()

    to_y(z, tokens).start()
    to_core(z, y, tokens).start()
    own = pltpu.make_async_copy(tokens, block(z, y, c), own_sem)
    own.start()
    gate_acc[...] = jnp.zeros_like(gate_acc)
    up_acc[...] = jnp.zeros_like(up_acc)

    def page_copy(i):
        other = (me + i) % group
        at = pl.ds(pl.multiple_of(other * units, 128), units)
        return remote(shrink.at[0, :, at], pages.at[me], page_s.at[i], page_r.at[me], {"tensor": other})

    def exp_copy(i):
        other = (me + i) % group
        at = pl.ds(pl.multiple_of(other * piece, piece), piece)
        return remote(expand.at[0, :, at], expand_pages.at[me], exp_s.at[i], exp_r.at[me], {"tensor": other})

    def page_arrived(i):
        other = (me + i) % group
        remote(pages.at[other], pages.at[other], page_s.at[i], page_r.at[other], core_dev).wait_recv()

    def exp_arrived(i):
        other = (me + i) % group
        remote(expand_pages.at[other], expand_pages.at[other], exp_s.at[i], exp_r.at[other], core_dev).wait_recv()

    own_pages = pltpu.make_async_copy(
        shrink.at[0, :, pl.ds(pl.multiple_of(me * units, 128), units)], pages.at[me], page_r.at[me])
    own_exp = pltpu.make_async_copy(
        expand.at[0, :, pl.ds(pl.multiple_of(me * piece, piece), piece)], expand_pages.at[me], exp_r.at[me])

    def z_round(k):
        @pl.when(z - k >= 0)
        def _():
            arrived(z - k, y, c)

            @pl.when(z < 3)
            def _():
                to_up(z - k).start()

            to_y(z - k).start()
            to_core(z - k, y).start()

        @pl.when(z + k <= 3)
        def _():
            arrived(z + k, y, c)

            @pl.when(z > 0)
            def _():
                to_dn(z + k).start()

            to_y(z + k).start()
            to_core(z + k, y).start()

    def y_round(j):
        z_ = near_first(z, j)
        arrived(z_, 1 - y, c)
        to_core(z_, 1 - y).start()

    @pl.loop(0, 8)
    def _(step):
        for at, act in (
            (0, lambda: own.wait()),
            (1, lambda: z_round(1)),
            (2, lambda: y_round(0)),
            (3, lambda: z_round(2)),
            (4, lambda: y_round(1)),
            (5, lambda: z_round(3)),
            (6, lambda: y_round(2)),
            (7, lambda: y_round(3)),
        ):
            pl.when(step == at)(act)

        @pl.when(step == page_step)
        def _():
            own_pages.start()
            own_exp.start()

            @pl.loop(1, group)
            def _(i):
                page_copy(i).start()
                exp_copy(i).start()

        pair = pair_of(step)
        arrived(pair // 2, pair % 2, 1 - c)
        slot = step % weight_slots
        for copy in weights(step):
            copy.wait()
        here = tok[pair]
        gate_acc[...] += jnp.dot(here, gate_w[slot], preferred_element_type=f32)
        up_acc[...] += jnp.dot(here, up_w[slot], preferred_element_type=f32)

        @pl.when(step + weight_slots < 8)
        def _():
            for copy in weights(step + weight_slots):
                copy.start()

        @pl.when(step == 7 - weight_slots + 1)
        def _():
            for q in range(down_slots):
                down_copy(q).start()

    gate_val = gate_acc[...]
    hid[...] = (gate_val / (1.0 + jnp.exp(-gate_val)) * up_acc[...]).astype(bf16)

    def core_copy(g):
        return remote(core_send.at[g], core_recv.at[g], core_s.at[g], core_r.at[g], core_dev)

    def y_copy(j):
        return remote(y_send.at[j], y_recv.at[j], y_s.at[j], y_r.at[j], y_dev)

    def chip_sum(g):
        core_copy(g).wait_recv()
        total = keep[g] + core_recv[g].astype(f32)

        @pl.when(g < 4)
        def _():
            y_send[g % 4] = total.astype(bf16)
            y_copy(g % 4).start()

        @pl.when(g >= 4)
        def _():
            keep[g] = total

    @pl.loop(0, 16)
    def _(q):
        g, sub = q // 2, q % 2
        down_copy(q).wait()
        part = jnp.dot(hid[...], down_w[q % down_slots], preferred_element_type=f32)

        @pl.when(q + down_slots < 16)
        def _():
            down_copy(q + down_slots).start()

        @pl.when(sub == 0)
        def _():
            core_send[g] = part.astype(bf16)
            core_copy(g).start()

            @pl.when(g > 0)
            def _():
                chip_sum(jnp.maximum(g - 1, 0))

        @pl.when(sub == 1)
        def _():
            keep[g] = part

    chip_sum(jnp.int32(7))

    own_pages.wait()
    own_exp.wait()

    @pl.loop(1, group)
    def _(i):
        page_arrived(i)
        exp_arrived(i)

    count = store_row.shape[1]
    hot = (ids[...] == lax.broadcasted_iota(jnp.int32, (rows, count), 1)).astype(f32)
    slot_row = lax.dot_general(
        jnp.broadcast_to(store_row[...].astype(f32), (8, count)), hot, NT,
        preferred_element_type=f32)[:1]
    store_at = lax.broadcasted_iota(jnp.int32, (group * rank, rows), 0) // rank
    chosen = store_at.astype(f32) == slot_row
    every = lax.dot_general(
        pages[...].reshape(group * rank, units), hid[...], NT, preferred_element_type=f32)
    mine = jnp.sum(jnp.where(chosen, every, 0.0).reshape(group, rank, rows), axis=0)
    sh_send[...] = mine

    def sh_copy(i):
        other = (me + i) % group
        return remote(sh_send, sh_recv.at[me], sh_s.at[i], sh_r.at[me], {"tensor": other})

    @pl.loop(1, group)
    def _(i):
        sh_copy(i).start()

    sh_recv[me] = mine

    def z_copy(z_, upward):
        if upward:
            return remote(z_send.at[z_], up_recv.at[z_], z_s.at[z_], up_r.at[z_], above)
        return remote(z_send.at[z_], dn_recv.at[z_], z_s.at[z_], dn_r.at[z_], below)

    for j in range(3):
        z_ = near_first(z, 3 - j)
        y_copy(j).wait_recv()
        keep[4 + j] += y_recv[j].astype(f32)

        @pl.when(z_ > z)
        def _():
            @pl.when(z > 0)
            def _():
                z_copy(z_, True).wait_recv()
                keep[4 + j] += up_recv[z_].astype(f32)

            z_send[z_] = keep[4 + j].astype(bf16)
            z_copy(z_, True).start()

        @pl.when(z_ < z)
        def _():
            @pl.when(z < 3)
            def _():
                z_copy(z_, False).wait_recv()
                keep[4 + j] += dn_recv[z_].astype(f32)

            z_send[z_] = keep[4 + j].astype(bf16)
            z_copy(z_, False).start()

    @pl.loop(1, group)
    def _(i):
        other = (me + i) % group
        remote(sh_recv.at[other], sh_recv.at[other], sh_s.at[i], sh_r.at[other], core_dev).wait_recv()

    shrink_sum = jnp.sum(sh_recv[...], axis=0)
    spread = jnp.where(
        chosen, jnp.broadcast_to(shrink_sum[None], (group, rank, rows)).reshape(group * rank, rows), 0.0).T
    flat_expand = expand_pages[...].reshape(group * rank, piece)
    spread_high = spread.astype(bf16)
    spread_low = (spread - spread_high.astype(f32)).astype(bf16)
    delta = jnp.dot(spread_high, flat_expand, preferred_element_type=f32) + jnp.dot(
        spread_low, flat_expand, preferred_element_type=f32)
    keep[7] += adapter_scale * delta
    y_copy(3).wait_recv()
    keep[7] += y_recv[3].astype(f32)

    @pl.when(z > 0)
    def _():
        z_copy(z, True).wait_recv()
        keep[7] += up_recv[z].astype(f32)

    @pl.when(z < 3)
    def _():
        z_copy(z, False).wait_recv()
        keep[7] += dn_recv[z].astype(f32)

    out[...] = keep[7].astype(bf16)

    for z_ in range(layers):
        for y_ in range(2):
            to_core(z_, y_).wait_send()
        to_y(z_).wait_send()

        @pl.when((z < 3) & (z_ <= z))
        def _():
            to_up(z_).wait_send()

        @pl.when((z > 0) & (z_ >= z))
        def _():
            to_dn(z_).wait_send()

        y_copy(z_).wait_send()

        @pl.when(z_ != z)
        def _():
            z_copy(z_, True).wait_send()

    for g in range(8):
        core_copy(g).wait_send()

    @pl.loop(1, group)
    def _(i):
        page_copy(i).wait_send()
        exp_copy(i).wait_send()
        sh_copy(i).wait_send()


page_step = 5


def local_fused(tokens, gate, up, down, shrink, expand, ids, store_row):
    rows, piece = tokens.shape
    units = gate.shape[1]
    rank = shrink.shape[1]
    vmem, dma = pltpu.VMEM, pltpu.SemaphoreType.DMA
    return pl.pallas_call(
        fused,
        out_shape=jax.ShapeDtypeStruct((rows, piece), bf16),
        in_specs=[pl.BlockSpec(memory_space=pltpu.VMEM)]
        + [pl.BlockSpec(memory_space=pl.ANY)] * 5
        + [pl.BlockSpec(memory_space=pltpu.VMEM)] * 2,
        out_specs=pl.BlockSpec(memory_space=pltpu.VMEM),
        scratch_shapes=[
            vmem((8, rows, 2 * piece), bf16),
            vmem((weight_slots, 2 * piece, units), bf16),
            vmem((weight_slots, 2 * piece, units), bf16),
            vmem((down_slots, units, piece), bf16),
            vmem((rows, units), f32),
            vmem((rows, units), f32),
            vmem((rows, units), bf16),
            vmem((group, rank, units), bf16),
            vmem((group, rank, piece), bf16),
            vmem((8, rows, piece), bf16),
            vmem((8, rows, piece), bf16),
            vmem((8, rows, piece), f32),
            vmem((4, rows, piece), bf16),
            vmem((4, rows, piece), bf16),
            vmem((4, rows, piece), bf16),
            vmem((4, rows, piece), bf16),
            vmem((4, rows, piece), bf16),
            vmem((rank, rows), f32),
            vmem((group, rank, rows), f32),
            dma((16,)), dma((8,)), dma((4,)), dma((4,)), dma((4,)), dma,
            dma((weight_slots,)), dma((weight_slots,)), dma((down_slots,)),
            dma((8,)), dma((8,)), dma((4,)), dma((4,)), dma((4,)), dma((4,)), dma((4,)),
            dma((16,)), dma((16,)), dma((16,)), dma((16,)), dma((16,)), dma((16,)),
        ],
        compiler_params=pltpu.CompilerParams(
            collective_id=0, has_side_effects=True, vmem_limit_bytes=63 * 2**20),
        cost_estimate=pl.CostEstimate(
            flops=6 * rows * 16 * piece * units, bytes_accessed=6 * 16 * piece * units, transcendentals=rows * units),
    )(tokens, gate, up, down, shrink, expand, ids, store_row.reshape(1, -1))


def pick(mesh_size):
    def run(tokens, gate, *rest):
        rows, piece = tokens.shape
        fits = mesh_size == group and rows % 128 == 0 and piece % 128 == 0 and gate.shape[1] % 128 == 0
        fits = fits and rest[2].shape[0] == 1 and rest[2].shape[1] == 16
        return (local_fused if fits else local)(tokens, gate, *rest)

    return run


def solution(mesh):
    placed = (
        P("replica", "tensor"),
        P(None, "tensor"),
        P(None, "tensor"),
        P("tensor", None),
        P("tensor", None, None),
        P("tensor", None, None),
        P("replica", None),
        P(),
    )
    return jax.shard_map(
        pick(mesh.shape["tensor"]), mesh=mesh, in_specs=placed, out_specs=P("replica", "tensor"), check_vma=False
    )
```

```python
import functools

import jax
import jax.numpy as jnp
from jax import lax
from jax.experimental import pallas as pl
from jax.experimental.pallas import tpu as pltpu
from jax.sharding import PartitionSpec as P

adapter_scale = 2.0


def local(
    tokens,
    gate_matrix,
    up_matrix,
    down_matrix,
    adapter_shrink_factors,
    adapter_expand_factors,
    request_adapter_ids,
    adapter_store_row,
):
    row_count = tokens.shape[0]
    feature_piece = lax.all_gather(tokens, "tensor", axis=1, tiled=True)
    gate_proj = jnp.dot(feature_piece, gate_matrix, preferred_element_type=jnp.float32)
    up_proj = jnp.dot(feature_piece, up_matrix, preferred_element_type=jnp.float32)
    hidden = (jax.nn.silu(gate_proj) * up_proj).astype(jnp.bfloat16)
    shrink_pages, expand_pages = (
        lax.all_to_all(adapter_shrink_factors, "tensor", split_axis=2, concat_axis=0, tiled=True),
        lax.all_to_all(adapter_expand_factors, "tensor", split_axis=2, concat_axis=0, tiled=True),
    )
    store_count = shrink_pages.shape[0]
    rank_size = shrink_pages.shape[1]
    store_row_ids = adapter_store_row[request_adapter_ids[:, 0]]
    selector = (store_row_ids[:, None] == jnp.arange(store_count, dtype=jnp.int32)[None, :]).astype(
        jnp.float32
    )
    flat_shrink = shrink_pages.reshape(store_count * rank_size, shrink_pages.shape[2])
    every_shrink = jnp.dot(hidden, flat_shrink.T, preferred_element_type=jnp.float32).reshape(
        row_count, store_count, rank_size
    )
    shrink_part = jnp.sum(every_shrink * selector[:, :, None], axis=1)
    shrink_product = lax.psum(shrink_part, "tensor")
    spread_shrink = (selector[:, :, None] * shrink_product[:, None, :]).reshape(
        row_count, store_count * rank_size
    )
    flat_expand = expand_pages.reshape(store_count * rank_size, expand_pages.shape[2]).astype(
        jnp.float32
    )
    adapter_delta = jnp.dot(
        spread_shrink,
        flat_expand,
        precision=lax.Precision.HIGHEST,
        preferred_element_type=jnp.float32,
    )
    partial_out = jnp.dot(hidden, down_matrix, preferred_element_type=jnp.float32)
    base_output = lax.psum_scatter(partial_out, "tensor", scatter_dimension=1, tiled=True)
    return (base_output + adapter_scale * adapter_delta).astype(jnp.bfloat16)


layers = 4
group = 16
weight_slots = 3
down_slots = 6
f32 = jnp.float32
bf16 = jnp.bfloat16
NT = (((1,), (1,)), ((), ()))


def near_first(z, j):
    low = jnp.where(z == 0, j, jnp.where(j < 2, 1 - j, j))
    w = 3 - z
    high = jnp.where(w == 0, j, jnp.where(j < 2, 1 - j, j))
    return jnp.where(z < 2, low, 3 - high)


def fused(
    tokens, gate, up, down, shrink, expand, ids, store_row, out,
    tok, gate_w, up_w, down_w, gate_acc, up_acc, hid, pages, expand_pages,
    core_send, core_recv, keep, y_send, y_recv, z_send, up_recv, dn_recv, sh_send, sh_recv,
    tok_recv_sem, tok_core_sem, tok_y_sem, tok_up_sem, tok_dn_sem, own_sem,
    gate_sem, up_sem, down_sem,
    core_s, core_r, y_s, y_r, z_s, up_r, dn_r,
    page_s, page_r, exp_s, exp_r, sh_s, sh_r, x_s, x_r,
):
    me = lax.axis_index("tensor")
    c, y, z = me % 2, (me // 2) % 2, me // 4
    piece = tokens.shape[1]
    units = hid.shape[1]
    rows = tokens.shape[0]
    rank = shrink.shape[1]

    def dev(z_, y_, c_):
        return {"tensor": 4 * z_ + 2 * y_ + c_}

    core_dev = dev(z, y, 1 - c)
    y_dev = dev(z, 1 - y, c)
    above = dev(jnp.minimum(z + 1, 3), y, c)
    below = dev(jnp.maximum(z - 1, 0), y, c)

    def remote(src, dst, s, r, device):
        return pltpu.make_async_remote_copy(
            src_ref=src, dst_ref=dst, send_sem=s, recv_sem=r,
            device_id=device, device_id_type=pl.DeviceIdType.MESH)

    def pair_of(step):
        second = jnp.where(step == 0, 0, jnp.where(step == 7, 1, 1 - step % 2))
        at = jnp.where(step == 7, 3, jnp.where(step % 2 == 1, (step + 1) // 2, jnp.maximum(step // 2 - 1, 0)))
        y_ = jnp.where(second == 1, 1 - y, y)
        return 2 * near_first(z, at) + y_

    def weights(step):
        slot = step % weight_slots
        at = pl.ds(pl.multiple_of(pair_of(step) * 2 * piece, 2 * piece), 2 * piece)
        return (
            pltpu.make_async_copy(gate.at[at, :], gate_w.at[slot], gate_sem.at[slot]),
            pltpu.make_async_copy(up.at[at, :], up_w.at[slot], up_sem.at[slot]),
        )

    def target(q):
        g, sub = q // 2, q % 2
        z_ = near_first(z, 3 - g % 4)
        y_ = jnp.where(g < 4, 1 - y, y)
        c_ = jnp.where(sub == 0, 1 - c, c)
        return 4 * z_ + 2 * y_ + c_

    def down_copy(q):
        slot = q % down_slots
        at = pl.ds(pl.multiple_of(target(q) * piece, piece), piece)
        return pltpu.make_async_copy(down.at[:, at], down_w.at[slot], down_sem.at[slot])

    for step in range(weight_slots):
        for copy in weights(step):
            copy.start()

    barrier = pltpu.get_barrier_semaphore()

    @pl.loop(1, group)
    def _(i):
        pl.semaphore_signal(barrier, inc=1, device_id={"tensor": (me + i) % group}, device_id_type=pl.DeviceIdType.MESH)

    pl.semaphore_signal(
        barrier, inc=1, device_id={"replica": 1 - lax.axis_index("replica")}, device_id_type=pl.DeviceIdType.MESH)
    pl.semaphore_wait(barrier, group)

    part = rows // 2

    def half(h):
        return pl.ds(h * part, part)

    def block(z_, y_, c_, h):
        return tok.at[2 * z_ + y_, half(h), pl.ds(pl.multiple_of(c_ * piece, piece), piece)]

    def tok_copy(z_, y_, c_, h, sem, device, own):
        ref = block(z_, y_, c_, h)
        t = 4 * z_ + 2 * y_ + c_
        return remote(tokens.at[half(h), :] if own else ref, ref, sem, tok_recv_sem.at[2 * t + h], device)

    def to_core(z_, y_, h, own=False):
        return tok_copy(z_, y_, c, h, tok_core_sem.at[4 * z_ + 2 * y_ + h], core_dev, own)

    def to_y(z_, h, own=False):
        return tok_copy(z_, y, c, h, tok_y_sem.at[2 * z_ + h], y_dev, own)

    def to_up(z_, h, own=False):
        return tok_copy(z_, y, c, h, tok_up_sem.at[2 * z_ + h], above, own)

    def to_dn(z_, h, own=False):
        return tok_copy(z_, y, c, h, tok_dn_sem.at[2 * z_ + h], below, own)

    def arrived(z_, y_, c_, h):
        tok_copy(z_, y_, c_, h, tok_up_sem.at[0], core_dev, False).wait_recv()

    for h in range(2):
        @pl.when(z < 3)
        def _():
            to_up(z, h, True).start()

        @pl.when(z > 0)
        def _():
            to_dn(z, h, True).start()

        to_y(z, h, True).start()

    for h in range(2):
        to_core(z, y, h, True).start()

    own = pltpu.make_async_copy(
        tokens, tok.at[2 * z + y, :, pl.ds(pl.multiple_of(c * piece, piece), piece)], own_sem)
    own.start()
    gate_acc[...] = jnp.zeros_like(gate_acc)
    up_acc[...] = jnp.zeros_like(up_acc)

    r = lax.axis_index("replica")
    x_dev = {"replica": 1 - r}
    page_width, exp_width = units // 2, piece // 2
    page_at = pl.ds(pl.multiple_of(r * page_width, 128), page_width)
    exp_at = pl.ds(pl.multiple_of(r * exp_width, 128), exp_width)

    def page_source(t):
        return shrink.at[0, :, pl.ds(pl.multiple_of(t * units + r * page_width, 128), page_width)]

    def exp_source(t):
        return expand.at[0, :, pl.ds(pl.multiple_of(t * piece + r * exp_width, 128), exp_width)]

    def page_copy(i):
        other = (me + i) % group
        return remote(page_source(other), pages.at[me, :, page_at], page_s.at[i], page_r.at[me], {"tensor": other})

    def exp_copy(i):
        other = (me + i) % group
        return remote(exp_source(other), expand_pages.at[me, :, exp_at], exp_s.at[i], exp_r.at[me], {"tensor": other})

    def page_arrived(i):
        other = (me + i) % group
        ref = pages.at[other, :, page_at]
        remote(ref, ref, page_s.at[i], page_r.at[other], core_dev).wait_recv()

    def exp_arrived(i):
        other = (me + i) % group
        ref = expand_pages.at[other, :, exp_at]
        remote(ref, ref, exp_s.at[i], exp_r.at[other], core_dev).wait_recv()

    own_pages = pltpu.make_async_copy(page_source(me), pages.at[me, :, page_at], page_r.at[me])
    own_exp = pltpu.make_async_copy(exp_source(me), expand_pages.at[me, :, exp_at], exp_r.at[me])
    x_pages = remote(pages.at[:, :, page_at], pages.at[:, :, page_at], x_s.at[0], x_r.at[0], x_dev)
    x_exp = remote(expand_pages.at[:, :, exp_at], expand_pages.at[:, :, exp_at], x_s.at[1], x_r.at[1], x_dev)

    def z_round(k, h):
        def lower():
            arrived(z - k, y, c, h)

            @pl.when(z < 3)
            def _():
                to_up(z - k, h).start()

            to_y(z - k, h).start()
            to_core(z - k, y, h).start()

        def upper():
            arrived(z + k, y, c, h)

            @pl.when(z > 0)
            def _():
                to_dn(z + k, h).start()

            to_y(z + k, h).start()
            to_core(z + k, y, h).start()

        pl.when((z >= 2) & (z + k <= 3))(upper)
        pl.when(z - k >= 0)(lower)
        pl.when((z < 2) & (z + k <= 3))(upper)

    def y_round(j, h):
        z_ = near_first(z, j)
        arrived(z_, 1 - y, c, h)
        to_core(z_, 1 - y, h).start()

    @pl.loop(0, 8)
    def _(step):
        @pl.when(step == 0)
        def _():
            own.wait()

        @pl.when(step == 1)
        def _():
            for h in range(2):
                z_round(1, h)
                y_round(0, h)

        for at in range(2, 6):
            @pl.when(step == at)
            def _():
                z_round(at // 2 + 1, at % 2)
                y_round(at // 2, at % 2)

        for h in range(2):
            @pl.when(step == 6 + h)
            def _():
                y_round(3, h)

        @pl.when(step == page_step)
        def _():
            own_pages.start()
            own_exp.start()

            @pl.loop(1, group)
            def _(i):
                page_copy(i).start()
                exp_copy(i).start()

        pair = pair_of(step)
        for h in range(2):
            arrived(pair // 2, pair % 2, 1 - c, h)
        slot = step % weight_slots
        for copy in weights(step):
            copy.wait()
        here = tok[pair]
        gate_acc[...] += jnp.dot(here, gate_w[slot], preferred_element_type=f32)
        up_acc[...] += jnp.dot(here, up_w[slot], preferred_element_type=f32)

        @pl.when(step + weight_slots < 8)
        def _():
            for copy in weights(step + weight_slots):
                copy.start()

        @pl.when(step == 7 - weight_slots + 1)
        def _():
            for q in range(down_slots):
                down_copy(q).start()

    gate_val = gate_acc[...]
    hid[...] = (gate_val / (1.0 + jnp.exp(-gate_val)) * up_acc[...]).astype(bf16)

    def core_copy(g):
        return remote(core_send.at[g], core_recv.at[g], core_s.at[g], core_r.at[g], core_dev)

    def y_copy(j, h):
        return remote(y_send.at[j, half(h), :], y_recv.at[j, half(h), :], y_s.at[2 * j + h], y_r.at[2 * j + h], y_dev)

    def chip_sum(g):
        core_copy(g).wait_recv()
        total = keep[g] + core_recv[g].astype(f32)

        @pl.when(g < 4)
        def _():
            y_send[g % 4] = total.astype(bf16)
            for h in range(2):
                y_copy(g % 4, h).start()

        @pl.when(g >= 4)
        def _():
            keep[g] = total

    @pl.loop(0, 16)
    def _(q):
        g, sub = q // 2, q % 2
        down_copy(q).wait()
        part = jnp.dot(hid[...], down_w[q % down_slots], preferred_element_type=f32)

        @pl.when(q + down_slots < 16)
        def _():
            down_copy(q + down_slots).start()

        @pl.when(sub == 0)
        def _():
            core_send[g] = part.astype(bf16)
            core_copy(g).start()

            @pl.when(g > 0)
            def _():
                chip_sum(jnp.maximum(g - 1, 0))

        @pl.when(sub == 1)
        def _():
            keep[g] = part

    chip_sum(jnp.int32(7))

    def z_copy(z_, h, upward):
        at = 2 * z_ + h
        src = z_send.at[z_, half(h), :]
        if upward:
            return remote(src, up_recv.at[z_, half(h), :], z_s.at[at], up_r.at[at], above)
        return remote(src, dn_recv.at[z_, half(h), :], z_s.at[at], dn_r.at[at], below)

    def add(g, h, ref):
        keep[g, half(h), :] += ref[half(h), :].astype(f32)

    def z_stage(j, h):
        z_ = near_first(z, 3 - j)
        y_copy(j, h).wait_recv()
        add(4 + j, h, y_recv.at[j])

        @pl.when(z_ > z)
        def _():
            @pl.when(z > 0)
            def _():
                z_copy(z_, h, True).wait_recv()
                add(4 + j, h, up_recv.at[z_])

            z_send[z_, half(h), :] = keep[4 + j, half(h), :].astype(bf16)
            z_copy(z_, h, True).start()

        @pl.when(z_ < z)
        def _():
            @pl.when(z < 3)
            def _():
                z_copy(z_, h, False).wait_recv()
                add(4 + j, h, dn_recv.at[z_])

            z_send[z_, half(h), :] = keep[4 + j, half(h), :].astype(bf16)
            z_copy(z_, h, False).start()

    z_stage(0, 0)

    own_pages.wait()
    own_exp.wait()

    @pl.loop(1, group)
    def _(i):
        page_arrived(i)
        exp_arrived(i)

    x_pages.start()
    x_exp.start()
    z_stage(0, 1)
    z_stage(1, 0)
    z_stage(1, 1)
    x_pages.wait_recv()
    x_exp.wait_recv()
    count = store_row.shape[1]
    hot = (ids[...] == lax.broadcasted_iota(jnp.int32, (rows, count), 1)).astype(f32)
    slot_row = lax.dot_general(
        jnp.broadcast_to(store_row[...].astype(f32), (8, count)), hot, NT,
        preferred_element_type=f32)[:1]
    store_at = lax.broadcasted_iota(jnp.int32, (group * rank, rows), 0) // rank
    chosen = store_at.astype(f32) == slot_row
    every = lax.dot_general(
        pages[...].reshape(group * rank, units), hid[...], NT, preferred_element_type=f32)
    mine = jnp.sum(jnp.where(chosen, every, 0.0).reshape(group, rank, rows), axis=0)
    sh_send[...] = mine

    def sh_copy(i):
        other = (me + i) % group
        return remote(sh_send, sh_recv.at[me], sh_s.at[i], sh_r.at[me], {"tensor": other})

    @pl.loop(1, group)
    def _(i):
        sh_copy(i).start()

    sh_recv[me] = mine
    z_stage(2, 0)
    z_stage(2, 1)

    @pl.loop(1, group)
    def _(i):
        other = (me + i) % group
        remote(sh_recv.at[other], sh_recv.at[other], sh_s.at[i], sh_r.at[other], core_dev).wait_recv()

    shrink_sum = jnp.sum(sh_recv[...], axis=0)
    spread = jnp.where(
        chosen, jnp.broadcast_to(shrink_sum[None], (group, rank, rows)).reshape(group * rank, rows), 0.0).T
    flat_expand = expand_pages[...].reshape(group * rank, piece)
    spread_high = spread.astype(bf16)
    spread_low = (spread - spread_high.astype(f32)).astype(bf16)
    delta = jnp.dot(spread_high, flat_expand, preferred_element_type=f32) + jnp.dot(
        spread_low, flat_expand, preferred_element_type=f32)
    keep[7] += adapter_scale * delta
    for h in range(2):
        @pl.when(z > 0)
        def _():
            z_copy(z, h, True).wait_recv()
            add(7, h, up_recv.at[z])

        @pl.when(z < 3)
        def _():
            z_copy(z, h, False).wait_recv()
            add(7, h, dn_recv.at[z])

    for h in range(2):
        y_copy(3, h).wait_recv()
        out[half(h), :] = (keep[7, half(h), :] + y_recv[3, half(h), :].astype(f32)).astype(bf16)

    x_pages.wait_send()
    x_exp.wait_send()
    for z_ in range(layers):
        for h in range(2):
            for y_ in range(2):
                to_core(z_, y_, h).wait_send()
            to_y(z_, h).wait_send()

            @pl.when((z < 3) & (z_ <= z))
            def _():
                to_up(z_, h).wait_send()

            @pl.when((z > 0) & (z_ >= z))
            def _():
                to_dn(z_, h).wait_send()

            y_copy(z_, h).wait_send()

            @pl.when(z_ != z)
            def _():
                z_copy(z_, h, True).wait_send()

    for g in range(8):
        core_copy(g).wait_send()

    @pl.loop(1, group)
    def _(i):
        page_copy(i).wait_send()
        exp_copy(i).wait_send()
        sh_copy(i).wait_send()


page_step = 7


def local_fused(tokens, gate, up, down, shrink, expand, ids, store_row):
    rows, piece = tokens.shape
    units = gate.shape[1]
    rank = shrink.shape[1]
    vmem, dma = pltpu.VMEM, pltpu.SemaphoreType.DMA
    return pl.pallas_call(
        fused,
        out_shape=jax.ShapeDtypeStruct((rows, piece), bf16),
        in_specs=[pl.BlockSpec(memory_space=pltpu.VMEM)]
        + [pl.BlockSpec(memory_space=pl.ANY)] * 5
        + [pl.BlockSpec(memory_space=pltpu.VMEM)] * 2,
        out_specs=pl.BlockSpec(memory_space=pltpu.VMEM),
        scratch_shapes=[
            vmem((8, rows, 2 * piece), bf16),
            vmem((weight_slots, 2 * piece, units), bf16),
            vmem((weight_slots, 2 * piece, units), bf16),
            vmem((down_slots, units, piece), bf16),
            vmem((rows, units), f32),
            vmem((rows, units), f32),
            vmem((rows, units), bf16),
            vmem((group, rank, units), bf16),
            vmem((group, rank, piece), bf16),
            vmem((8, rows, piece), bf16),
            vmem((8, rows, piece), bf16),
            vmem((8, rows, piece), f32),
            vmem((4, rows, piece), bf16),
            vmem((4, rows, piece), bf16),
            vmem((4, rows, piece), bf16),
            vmem((4, rows, piece), bf16),
            vmem((4, rows, piece), bf16),
            vmem((rank, rows), f32),
            vmem((group, rank, rows), f32),
            dma((32,)), dma((16,)), dma((8,)), dma((8,)), dma((8,)), dma,
            dma((weight_slots,)), dma((weight_slots,)), dma((down_slots,)),
            dma((8,)), dma((8,)), dma((8,)), dma((8,)), dma((8,)), dma((8,)), dma((8,)),
            dma((16,)), dma((16,)), dma((16,)), dma((16,)), dma((16,)), dma((16,)), dma((2,)), dma((2,)),
        ],
        compiler_params=pltpu.CompilerParams(
            collective_id=0, has_side_effects=True, vmem_limit_bytes=63 * 2**20),
        cost_estimate=pl.CostEstimate(
            flops=6 * rows * 16 * piece * units, bytes_accessed=6 * 16 * piece * units, transcendentals=rows * units),
    )(tokens, gate, up, down, shrink, expand, ids, store_row.reshape(1, -1))


def pick(mesh_size, replicas):
    def run(tokens, gate, *rest):
        rows, piece = tokens.shape
        fits = (mesh_size, replicas) == (group, 2) and rows % 128 == 0 and piece % 256 == 0 and gate.shape[1] % 256 == 0
        fits = fits and rest[2].shape[0] == 1 and rest[2].shape[1] == 16
        return (local_fused if fits else local)(tokens, gate, *rest)

    return run


def solution(mesh):
    placed = (
        P("replica", "tensor"),
        P(None, "tensor"),
        P(None, "tensor"),
        P("tensor", None),
        P("tensor", None, None),
        P("tensor", None, None),
        P("replica", None),
        P(),
    )
    return jax.shard_map(
        pick(mesh.shape["tensor"], mesh.shape["replica"]), mesh=mesh, in_specs=placed, out_specs=P("replica", "tensor"), check_vma=False
    )
```

```python
import functools

import jax
import jax.numpy as jnp
from jax import lax
from jax.experimental import pallas as pl
from jax.experimental.pallas import tpu as pltpu
from jax.sharding import PartitionSpec as P

adapter_scale = 2.0


def local(
    tokens,
    gate_matrix,
    up_matrix,
    down_matrix,
    adapter_shrink_factors,
    adapter_expand_factors,
    request_adapter_ids,
    adapter_store_row,
):
    row_count = tokens.shape[0]
    feature_piece = lax.all_gather(tokens, "tensor", axis=1, tiled=True)
    gate_proj = jnp.dot(feature_piece, gate_matrix, preferred_element_type=jnp.float32)
    up_proj = jnp.dot(feature_piece, up_matrix, preferred_element_type=jnp.float32)
    hidden = (jax.nn.silu(gate_proj) * up_proj).astype(jnp.bfloat16)
    shrink_pages, expand_pages = (
        lax.all_to_all(adapter_shrink_factors, "tensor", split_axis=2, concat_axis=0, tiled=True),
        lax.all_to_all(adapter_expand_factors, "tensor", split_axis=2, concat_axis=0, tiled=True),
    )
    store_count = shrink_pages.shape[0]
    rank_size = shrink_pages.shape[1]
    store_row_ids = adapter_store_row[request_adapter_ids[:, 0]]
    selector = (store_row_ids[:, None] == jnp.arange(store_count, dtype=jnp.int32)[None, :]).astype(
        jnp.float32
    )
    flat_shrink = shrink_pages.reshape(store_count * rank_size, shrink_pages.shape[2])
    every_shrink = jnp.dot(hidden, flat_shrink.T, preferred_element_type=jnp.float32).reshape(
        row_count, store_count, rank_size
    )
    shrink_part = jnp.sum(every_shrink * selector[:, :, None], axis=1)
    shrink_product = lax.psum(shrink_part, "tensor")
    spread_shrink = (selector[:, :, None] * shrink_product[:, None, :]).reshape(
        row_count, store_count * rank_size
    )
    flat_expand = expand_pages.reshape(store_count * rank_size, expand_pages.shape[2]).astype(
        jnp.float32
    )
    adapter_delta = jnp.dot(
        spread_shrink,
        flat_expand,
        precision=lax.Precision.HIGHEST,
        preferred_element_type=jnp.float32,
    )
    partial_out = jnp.dot(hidden, down_matrix, preferred_element_type=jnp.float32)
    base_output = lax.psum_scatter(partial_out, "tensor", scatter_dimension=1, tiled=True)
    return (base_output + adapter_scale * adapter_delta).astype(jnp.bfloat16)


layers = 4
group = 16
weight_slots = 3
down_slots = 6
f32 = jnp.float32
bf16 = jnp.bfloat16
NT = (((1,), (1,)), ((), ()))


def near_first(z, j):
    low = jnp.where(z == 0, j, jnp.where(j < 2, 1 - j, j))
    w = 3 - z
    high = jnp.where(w == 0, j, jnp.where(j < 2, 1 - j, j))
    return jnp.where(z < 2, low, 3 - high)


def fused(
    tokens, gate, up, down, shrink, expand, ids, store_row, out,
    tok, gate_w, up_w, down_w, gate_acc, up_acc, hid, pages, expand_pages,
    core_send, core_recv, keep, y_send, y_recv, z_send, up_recv, dn_recv, sh_send, sh_recv,
    tok_recv_sem, tok_core_sem, tok_y_sem, tok_up_sem, tok_dn_sem, own_sem,
    gate_sem, up_sem, down_sem,
    core_s, core_r, y_s, y_r, z_s, up_r, dn_r,
    page_s, page_r, exp_s, exp_r, sh_s, sh_r, x_s, x_r,
):
    me = lax.axis_index("tensor")
    c, y, z = me % 2, (me // 2) % 2, me // 4
    piece = tokens.shape[1]
    units = hid.shape[1]
    rows = tokens.shape[0]
    rank = shrink.shape[1]

    def dev(z_, y_, c_):
        return {"tensor": 4 * z_ + 2 * y_ + c_}

    core_dev = dev(z, y, 1 - c)
    y_dev = dev(z, 1 - y, c)
    above = dev(jnp.minimum(z + 1, 3), y, c)
    below = dev(jnp.maximum(z - 1, 0), y, c)

    def remote(src, dst, s, r, device):
        return pltpu.make_async_remote_copy(
            src_ref=src, dst_ref=dst, send_sem=s, recv_sem=r,
            device_id=device, device_id_type=pl.DeviceIdType.MESH)

    def pair_of(step):
        second = jnp.where(step == 0, 0, jnp.where(step == 7, 1, 1 - step % 2))
        at = jnp.where(step == 7, 3, jnp.where(step % 2 == 1, (step + 1) // 2, jnp.maximum(step // 2 - 1, 0)))
        y_ = jnp.where(second == 1, 1 - y, y)
        return 2 * near_first(z, at) + y_

    def weights(step):
        slot = step % weight_slots
        at = pl.ds(pl.multiple_of(pair_of(step) * 2 * piece, 2 * piece), 2 * piece)
        return (
            pltpu.make_async_copy(gate.at[at, :], gate_w.at[slot], gate_sem.at[slot]),
            pltpu.make_async_copy(up.at[at, :], up_w.at[slot], up_sem.at[slot]),
        )

    def target(q):
        g, sub = q // 2, q % 2
        z_ = near_first(z, 3 - g % 4)
        y_ = jnp.where(g < 4, 1 - y, y)
        c_ = jnp.where(sub == 0, 1 - c, c)
        return 4 * z_ + 2 * y_ + c_

    def down_copy(q):
        slot = q % down_slots
        at = pl.ds(pl.multiple_of(target(q) * piece, piece), piece)
        return pltpu.make_async_copy(down.at[:, at], down_w.at[slot], down_sem.at[slot])

    for step in range(weight_slots):
        for copy in weights(step):
            copy.start()

    barrier = pltpu.get_barrier_semaphore()

    @pl.loop(1, group)
    def _(i):
        pl.semaphore_signal(barrier, inc=1, device_id={"tensor": (me + i) % group}, device_id_type=pl.DeviceIdType.MESH)

    pl.semaphore_signal(
        barrier, inc=1, device_id={"replica": 1 - lax.axis_index("replica")}, device_id_type=pl.DeviceIdType.MESH)
    gate_acc[...] = jnp.zeros_like(gate_acc)
    up_acc[...] = jnp.zeros_like(up_acc)
    pl.semaphore_wait(barrier, group)

    part = rows // 2

    def half(h):
        return pl.ds(h * part, part)

    def block(z_, y_, c_, h):
        return tok.at[2 * z_ + y_, half(h), pl.ds(pl.multiple_of(c_ * piece, piece), piece)]

    def tok_copy(z_, y_, c_, h, sem, device, own):
        ref = block(z_, y_, c_, h)
        t = 4 * z_ + 2 * y_ + c_
        return remote(tokens.at[half(h), :] if own else ref, ref, sem, tok_recv_sem.at[2 * t + h], device)

    def to_core(z_, y_, h, own=False):
        return tok_copy(z_, y_, c, h, tok_core_sem.at[4 * z_ + 2 * y_ + h], core_dev, own)

    def to_y(z_, h, own=False):
        return tok_copy(z_, y, c, h, tok_y_sem.at[2 * z_ + h], y_dev, own)

    def to_up(z_, h, own=False):
        return tok_copy(z_, y, c, h, tok_up_sem.at[2 * z_ + h], above, own)

    def to_dn(z_, h, own=False):
        return tok_copy(z_, y, c, h, tok_dn_sem.at[2 * z_ + h], below, own)

    def arrived(z_, y_, c_, h):
        tok_copy(z_, y_, c_, h, tok_up_sem.at[0], core_dev, False).wait_recv()

    for h in range(2):
        @pl.when(z < 3)
        def _():
            to_up(z, h, True).start()

        @pl.when(z > 0)
        def _():
            to_dn(z, h, True).start()

        to_y(z, h, True).start()

    for h in range(2):
        to_core(z, y, h, True).start()

    own = pltpu.make_async_copy(
        tokens, tok.at[2 * z + y, :, pl.ds(pl.multiple_of(c * piece, piece), piece)], own_sem)
    own.start()

    r = lax.axis_index("replica")
    x_dev = {"replica": 1 - r}
    page_width, exp_width = units // 2, piece // 2
    page_at = pl.ds(pl.multiple_of(r * page_width, 128), page_width)
    exp_at = pl.ds(pl.multiple_of(r * exp_width, 128), exp_width)

    def page_source(t):
        return shrink.at[0, :, pl.ds(pl.multiple_of(t * units + r * page_width, 128), page_width)]

    def exp_source(t):
        return expand.at[0, :, pl.ds(pl.multiple_of(t * piece + r * exp_width, 128), exp_width)]

    def page_copy(i):
        other = (me + i) % group
        return remote(page_source(other), pages.at[me, :, page_at], page_s.at[i], page_r.at[me], {"tensor": other})

    def exp_copy(i):
        other = (me + i) % group
        return remote(exp_source(other), expand_pages.at[me, :, exp_at], exp_s.at[i], exp_r.at[me], {"tensor": other})

    def page_arrived(i):
        other = (me + i) % group
        ref = pages.at[other, :, page_at]
        remote(ref, ref, page_s.at[i], page_r.at[other], core_dev).wait_recv()

    def exp_arrived(i):
        other = (me + i) % group
        ref = expand_pages.at[other, :, exp_at]
        remote(ref, ref, exp_s.at[i], exp_r.at[other], core_dev).wait_recv()

    own_pages = pltpu.make_async_copy(page_source(me), pages.at[me, :, page_at], page_r.at[me])
    own_exp = pltpu.make_async_copy(exp_source(me), expand_pages.at[me, :, exp_at], exp_r.at[me])
    x_pages = remote(pages.at[:, :, page_at], pages.at[:, :, page_at], x_s.at[0], x_r.at[0], x_dev)
    x_exp = remote(expand_pages.at[:, :, exp_at], expand_pages.at[:, :, exp_at], x_s.at[1], x_r.at[1], x_dev)

    def z_round(k, h):
        def lower():
            arrived(z - k, y, c, h)

            @pl.when(z < 3)
            def _():
                to_up(z - k, h).start()

            to_y(z - k, h).start()
            to_core(z - k, y, h).start()

        def upper():
            arrived(z + k, y, c, h)

            @pl.when(z > 0)
            def _():
                to_dn(z + k, h).start()

            to_y(z + k, h).start()
            to_core(z + k, y, h).start()

        pl.when((z >= 2) & (z + k <= 3))(upper)
        pl.when(z - k >= 0)(lower)
        pl.when((z < 2) & (z + k <= 3))(upper)

    def y_round(j, h):
        z_ = near_first(z, j)
        arrived(z_, 1 - y, c, h)
        to_core(z_, 1 - y, h).start()

    @pl.loop(0, 8)
    def _(step):
        @pl.when(step == 0)
        def _():
            own.wait()

        @pl.when(step == 1)
        def _():
            for h in range(2):
                z_round(1, h)
                y_round(0, h)

        for at in range(2, 6):
            @pl.when(step == at)
            def _():
                z_round(at // 2 + 1, at % 2)
                y_round(at // 2, at % 2)

        for h in range(2):
            @pl.when(step == 6 + h)
            def _():
                y_round(3, h)

        @pl.when(step == page_step)
        def _():
            own_pages.start()
            own_exp.start()

            @pl.loop(1, group)
            def _(i):
                page_copy(i).start()
                exp_copy(i).start()

        pair = pair_of(step)
        for h in range(2):
            arrived(pair // 2, pair % 2, 1 - c, h)
        slot = step % weight_slots
        for copy in weights(step):
            copy.wait()
        here = tok[pair]
        gate_acc[...] += jnp.dot(here, gate_w[slot], preferred_element_type=f32)
        up_acc[...] += jnp.dot(here, up_w[slot], preferred_element_type=f32)

        @pl.when(step + weight_slots < 8)
        def _():
            for copy in weights(step + weight_slots):
                copy.start()

        @pl.when(step == 7 - weight_slots + 1)
        def _():
            for q in range(down_slots):
                down_copy(q).start()

    gate_val = gate_acc[...]
    hid[...] = (gate_val / (1.0 + jnp.exp(-gate_val)) * up_acc[...]).astype(bf16)

    def core_copy(g):
        return remote(core_send.at[g], core_recv.at[g], core_s.at[g], core_r.at[g], core_dev)

    def y_copy(j, h):
        return remote(y_send.at[j, half(h), :], y_recv.at[j, half(h), :], y_s.at[2 * j + h], y_r.at[2 * j + h], y_dev)

    def chip_sum(g):
        core_copy(g).wait_recv()
        total = keep[g] + core_recv[g].astype(f32)

        @pl.when(g < 4)
        def _():
            y_send[g % 4] = total.astype(bf16)
            for h in range(2):
                y_copy(g % 4, h).start()

        @pl.when(g >= 4)
        def _():
            keep[g] = total

    @pl.loop(0, 16)
    def _(q):
        g, sub = q // 2, q % 2
        down_copy(q).wait()
        part = jnp.dot(hid[...], down_w[q % down_slots], preferred_element_type=f32)

        @pl.when(q + down_slots < 16)
        def _():
            down_copy(q + down_slots).start()

        @pl.when(sub == 0)
        def _():
            core_send[g] = part.astype(bf16)
            core_copy(g).start()

            @pl.when(g > 0)
            def _():
                chip_sum(jnp.maximum(g - 1, 0))

        @pl.when(sub == 1)
        def _():
            keep[g] = part

    chip_sum(jnp.int32(7))

    def z_copy(z_, h, upward):
        at = 2 * z_ + h
        src = z_send.at[z_, half(h), :]
        if upward:
            return remote(src, up_recv.at[z_, half(h), :], z_s.at[at], up_r.at[at], above)
        return remote(src, dn_recv.at[z_, half(h), :], z_s.at[at], dn_r.at[at], below)

    def add(g, h, ref):
        keep[g, half(h), :] += ref[half(h), :].astype(f32)

    def z_stage(j, h):
        z_ = near_first(z, 3 - j)
        y_copy(j, h).wait_recv()
        add(4 + j, h, y_recv.at[j])

        @pl.when(z_ > z)
        def _():
            @pl.when(z > 0)
            def _():
                z_copy(z_, h, True).wait_recv()
                add(4 + j, h, up_recv.at[z_])

            z_send[z_, half(h), :] = keep[4 + j, half(h), :].astype(bf16)
            z_copy(z_, h, True).start()

        @pl.when(z_ < z)
        def _():
            @pl.when(z < 3)
            def _():
                z_copy(z_, h, False).wait_recv()
                add(4 + j, h, dn_recv.at[z_])

            z_send[z_, half(h), :] = keep[4 + j, half(h), :].astype(bf16)
            z_copy(z_, h, False).start()

    z_stage(0, 0)

    own_pages.wait()
    own_exp.wait()

    @pl.loop(1, group)
    def _(i):
        page_arrived(i)
        exp_arrived(i)

    x_pages.start()
    x_exp.start()
    z_stage(0, 1)
    z_stage(1, 0)
    z_stage(1, 1)
    x_pages.wait_recv()
    x_exp.wait_recv()
    count = store_row.shape[1]
    hot = (ids[...] == lax.broadcasted_iota(jnp.int32, (count, rows), 0)).astype(f32)
    slot_row = jnp.dot(
        jnp.broadcast_to(store_row[...].astype(f32), (8, count)), hot, preferred_element_type=f32)[:1]
    store_at = lax.broadcasted_iota(jnp.int32, (group * rank, rows), 0) // rank
    chosen = store_at.astype(f32) == slot_row
    every = lax.dot_general(
        pages[...].reshape(group * rank, units), hid[...], NT, preferred_element_type=f32)
    mine = jnp.sum(jnp.where(chosen, every, 0.0).reshape(group, rank, rows), axis=0)
    sh_send[...] = mine

    def sh_copy(i):
        other = (me + i) % group
        return remote(sh_send, sh_recv.at[me], sh_s.at[i], sh_r.at[me], {"tensor": other})

    @pl.loop(1, group)
    def _(i):
        sh_copy(i).start()

    sh_recv[me] = mine
    z_stage(2, 0)
    z_stage(2, 1)

    @pl.loop(1, group)
    def _(i):
        other = (me + i) % group
        remote(sh_recv.at[other], sh_recv.at[other], sh_s.at[i], sh_r.at[other], core_dev).wait_recv()

    shrink_sum = jnp.sum(sh_recv[...], axis=0)
    spread = jnp.where(
        chosen, jnp.broadcast_to(shrink_sum[None], (group, rank, rows)).reshape(group * rank, rows), 0.0).T
    flat_expand = expand_pages[...].reshape(group * rank, piece)
    spread_high = spread.astype(bf16)
    spread_low = (spread - spread_high.astype(f32)).astype(bf16)
    delta = jnp.dot(spread_high, flat_expand, preferred_element_type=f32) + jnp.dot(
        spread_low, flat_expand, preferred_element_type=f32)
    keep[7] += adapter_scale * delta
    for h in range(2):
        @pl.when(z > 0)
        def _():
            z_copy(z, h, True).wait_recv()
            add(7, h, up_recv.at[z])

        @pl.when(z < 3)
        def _():
            z_copy(z, h, False).wait_recv()
            add(7, h, dn_recv.at[z])

    for h in range(2):
        y_copy(3, h).wait_recv()
        out[half(h), :] = (keep[7, half(h), :] + y_recv[3, half(h), :].astype(f32)).astype(bf16)

    x_pages.wait_send()
    x_exp.wait_send()
    for z_ in range(layers):
        for h in range(2):
            for y_ in range(2):
                to_core(z_, y_, h).wait_send()
            to_y(z_, h).wait_send()

            @pl.when((z < 3) & (z_ <= z))
            def _():
                to_up(z_, h).wait_send()

            @pl.when((z > 0) & (z_ >= z))
            def _():
                to_dn(z_, h).wait_send()

            y_copy(z_, h).wait_send()

            @pl.when(z_ != z)
            def _():
                z_copy(z_, h, True).wait_send()

    for g in range(8):
        core_copy(g).wait_send()

    @pl.loop(1, group)
    def _(i):
        page_copy(i).wait_send()
        exp_copy(i).wait_send()
        sh_copy(i).wait_send()


page_step = 7


def local_fused(tokens, gate, up, down, shrink, expand, ids, store_row):
    rows, piece = tokens.shape
    units = gate.shape[1]
    rank = shrink.shape[1]
    vmem, dma = pltpu.VMEM, pltpu.SemaphoreType.DMA
    return pl.pallas_call(
        fused,
        out_shape=jax.ShapeDtypeStruct((rows, piece), bf16),
        in_specs=[pl.BlockSpec(memory_space=pltpu.VMEM)]
        + [pl.BlockSpec(memory_space=pl.ANY)] * 5
        + [pl.BlockSpec(memory_space=pltpu.VMEM)] * 2,
        out_specs=pl.BlockSpec(memory_space=pltpu.VMEM),
        scratch_shapes=[
            vmem((8, rows, 2 * piece), bf16),
            vmem((weight_slots, 2 * piece, units), bf16),
            vmem((weight_slots, 2 * piece, units), bf16),
            vmem((down_slots, units, piece), bf16),
            vmem((rows, units), f32),
            vmem((rows, units), f32),
            vmem((rows, units), bf16),
            vmem((group, rank, units), bf16),
            vmem((group, rank, piece), bf16),
            vmem((8, rows, piece), bf16),
            vmem((8, rows, piece), bf16),
            vmem((8, rows, piece), f32),
            vmem((4, rows, piece), bf16),
            vmem((4, rows, piece), bf16),
            vmem((4, rows, piece), bf16),
            vmem((4, rows, piece), bf16),
            vmem((4, rows, piece), bf16),
            vmem((rank, rows), f32),
            vmem((group, rank, rows), f32),
            dma((32,)), dma((16,)), dma((8,)), dma((8,)), dma((8,)), dma,
            dma((weight_slots,)), dma((weight_slots,)), dma((down_slots,)),
            dma((8,)), dma((8,)), dma((8,)), dma((8,)), dma((8,)), dma((8,)), dma((8,)),
            dma((16,)), dma((16,)), dma((16,)), dma((16,)), dma((16,)), dma((16,)), dma((2,)), dma((2,)),
        ],
        compiler_params=pltpu.CompilerParams(
            collective_id=0, has_side_effects=True, vmem_limit_bytes=63 * 2**20),
        cost_estimate=pl.CostEstimate(
            flops=6 * rows * 16 * piece * units, bytes_accessed=6 * 16 * piece * units, transcendentals=rows * units),
    )(tokens, gate, up, down, shrink, expand, ids.reshape(1, -1), store_row.reshape(1, -1))


def pick(mesh_size, replicas):
    def run(tokens, gate, *rest):
        rows, piece = tokens.shape
        fits = (mesh_size, replicas) == (group, 2) and rows % 128 == 0 and piece % 256 == 0 and gate.shape[1] % 256 == 0
        fits = fits and rest[2].shape[0] == 1 and rest[2].shape[1] == 16
        return (local_fused if fits else local)(tokens, gate, *rest)

    return run


def solution(mesh):
    placed = (
        P("replica", "tensor"),
        P(None, "tensor"),
        P(None, "tensor"),
        P("tensor", None),
        P("tensor", None, None),
        P("tensor", None, None),
        P("replica", None),
        P(),
    )
    return jax.shard_map(
        pick(mesh.shape["tensor"], mesh.shape["replica"]), mesh=mesh, in_specs=placed, out_specs=P("replica", "tensor"), check_vma=False
    )
```
